256 devices in a mesh: section: 2 (over core), dp: 8 (over x, y_hi), tensor: 16 (over y_lo, z).
Axes of the slice: x: 4, y: 4 (y_hi: 2, y_lo: 2; y = y_hi * 2 + y_lo), z: 8, core: 2. Of those that a mesh axis runs over, the one named last changes fastest.
Arguments:
- inputs: bfloat16 [2, 128, 8192], P(None, 'dp', 'tensor'), may hold values from -6 to 6
- cotangent: bfloat16 [2, 128, 8192], P(None, 'dp', 'tensor'), may hold values from -6 to 6
- scale_exps: int32 [2, 16, 64], P(None, 'dp', 'tensor'), may hold values from -9 to -6
- up_weight: bfloat16 [2, 8192, 20480], P('section', 'tensor', 'dp'), may hold values from -0.0625 to 0.0625
- down_weight: bfloat16 [2, 20480, 8192], P('section', 'dp', 'tensor'), may hold values from -0.0390625 to 0.0390625
Outputs:
- section_out: bfloat16 [2, 2, 128, 8192], P('section', None, 'dp', 'tensor')
- input_grads: bfloat16 [2, 2, 128, 8192], P('section', None, 'dp', 'tensor')
- up_grads: bfloat16 [2, 8192, 20480], P('section', 'tensor', 'dp')
- down_grads: bfloat16 [2, 20480, 8192], P('section', 'dp', 'tensor')
The draws below stay inside these ranges and needn't reach their ends.
All inputs are finite; a program needn't handle non-finite values.
Results may differ from the reference program's by a relative error of at most 0.039.
Values may be sent and summed in bfloat16 or wider, within the bound.
A program may use at most 128 MiB of HBM per device.

```python
import math
import jax
import jax.numpy as jnp
from jax import lax

D = 8192
FFW = 20480
TOK = 128
MB = 2
TILE_ROWS = 8
TILE_COLS = 128
BLOCKS = 16


def set_ends(drawn, own_key, low, largest):
    longest = drawn.shape.index(max(drawn.shape))
    spots = []
    for shift in (0, 1):
        where = [jax.random.randint(jax.random.fold_in(own_key, axis), (), 0, length) for axis, length in enumerate(drawn.shape)]
        where[longest] = (where[longest] + shift) % drawn.shape[longest]
        spots.append(tuple(where))
    return drawn.at[spots[0]].set(low).at[spots[1]].set(largest)


def block_scale(own_key, extent, split, low, high):
    loudness = 1.0
    for dim, parts in split:
        heights = jax.random.uniform(jax.random.fold_in(jax.random.fold_in(own_key, 6), dim), (parts,), jnp.float32, low / len(split), high / len(split))
        loudness = loudness * jnp.repeat(jnp.exp(heights), extent[dim] // parts).reshape((-1,) + (1,) * (len(extent) - 1 - dim))
    return loudness


def bell_draw(own_key, dims, spread, most, shards=(), held_as=jnp.bfloat16):
    values = jax.random.normal(own_key, dims, jnp.float32) * spread
    if len(shards) > 0:
        values = block_scale(own_key, dims, shards, -0.22, 0.18) * values
    return jnp.clip(values, min=-most, max=most).astype(held_as)


def setup_inputs(seed: int = 0) -> dict:
    arg_keys = jax.random.split(jax.random.key(seed), 6)
    return {
        "inputs": bell_draw(arg_keys[0], (MB, TOK, D), 1.0, 6.0, ((1, 8), (2, 16))),
        "cotangent": bell_draw(arg_keys[1], (MB, TOK, D), 1.0, 6.0, ((1, 8), (2, 16))),
        "scale_exps": set_ends(jax.random.randint(arg_keys[2], (MB, TOK // TILE_ROWS, D // TILE_COLS), -9, -5), jax.random.fold_in(arg_keys[2], 1), -9, (-5) - 1).astype(jnp.int32),
        "up_weight": bell_draw(arg_keys[3], (2, D, FFW), D ** -0.5, 0.0625, ((0, 2), (1, 16), (2, 8))),
        "down_weight": bell_draw(arg_keys[4], (2, FFW, D), FFW ** -0.5, 0.0390625, ((0, 2), (1, 8), (2, 16))),
    }


gelu_coef = math.sqrt(2.0 / math.pi)

def gelu_value(values):
    inner_arg = gelu_coef * (values + 0.044715 * values * values * values)
    return 0.5 * values * (1.0 + jnp.tanh(inner_arg))

def gelu_slope(values):
    tangent = jnp.tanh(gelu_coef * (values + 0.044715 * values * values * values))
    return 0.5 * (1.0 + tangent) + 0.5 * values * (1.0 - tangent * tangent) * gelu_coef * (1.0 + 3.0 * 0.044715 * values * values)

def round_trip(values):
    return lax.optimization_barrier(values.astype(jnp.bfloat16)).astype(jnp.float32)

def blockwise(left_rows, right_rows):
    block_width = left_rows.shape[1] // BLOCKS
    running = jnp.zeros((left_rows.shape[0], right_rows.shape[1]), jnp.float32)
    for block_index in range(BLOCKS):
        low = block_index * block_width
        block_term = jnp.dot(left_rows[:, low:low + block_width], right_rows[low:low + block_width], preferred_element_type=jnp.float32)
        running = running + round_trip(block_term)
    return running

def tile_factor(exponents, sign_value):
    factor = jnp.exp2(sign_value * exponents.astype(jnp.float32))
    return jnp.repeat(jnp.repeat(factor, TILE_ROWS, axis=0), TILE_COLS, axis=1)

def section_forward(section_input, w_up, w_down):
    hidden = blockwise(section_input, w_up)
    active = gelu_value(hidden).astype(jnp.bfloat16)
    result = (section_input.astype(jnp.float32) + jnp.dot(active, w_down, preferred_element_type=jnp.float32)).astype(jnp.bfloat16)
    return (hidden, active, result)

def section_backward(section_input, hidden, active, incoming, w_up, w_down):
    back_sum = blockwise(incoming, w_down.T)
    delta_local = (back_sum * gelu_slope(hidden)).astype(jnp.bfloat16)
    up_term = jnp.dot(section_input.T, delta_local, preferred_element_type=jnp.float32)
    down_term = jnp.dot(active.T, incoming, preferred_element_type=jnp.float32)
    through = incoming.astype(jnp.float32) + jnp.dot(delta_local, w_up.T, preferred_element_type=jnp.float32)
    return (through, up_term, down_term)

def reference(inputs, cotangent, scale_exps, up_weight, down_weight):
    first_outs, second_outs, first_grads, second_grads = ([], [], [], [])
    up_first = jnp.zeros(up_weight.shape[1:], jnp.float32)
    up_second = jnp.zeros(up_weight.shape[1:], jnp.float32)
    down_first = jnp.zeros(down_weight.shape[1:], jnp.float32)
    down_second = jnp.zeros(down_weight.shape[1:], jnp.float32)
    for micro_index in range(MB):
        first_input = inputs[micro_index]
        hidden_one, active_one, first_result = section_forward(first_input, up_weight[0], down_weight[0])
        hidden_two, active_two, second_result = section_forward(first_result, up_weight[1], down_weight[1])
        first_outs.append(first_result)
        second_outs.append(second_result)
        through_two, up_term, down_term = section_backward(first_result, hidden_two, active_two, cotangent[micro_index], up_weight[1], down_weight[1])
        up_second = up_second + up_term
        down_second = down_second + down_term
        second_grads.append(through_two.astype(jnp.bfloat16))
        exponents = scale_exps[micro_index]
        packed = jnp.clip(through_two * tile_factor(exponents, -1.0), -448.0, 448.0).astype(jnp.bfloat16)
        restored = (packed.astype(jnp.float32) * tile_factor(exponents, 1.0)).astype(jnp.bfloat16)
        through_one, up_term, down_term = section_backward(first_input, hidden_one, active_one, restored, up_weight[0], down_weight[0])
        up_first = up_first + up_term
        down_first = down_first + down_term
        first_grads.append(through_one.astype(jnp.bfloat16))
    section_out = jnp.stack([jnp.stack(first_outs), jnp.stack(second_outs)])
    input_grads = jnp.stack([jnp.stack(first_grads), jnp.stack(second_grads)])
    up_grads = jnp.stack([up_first, up_second]).astype(jnp.bfloat16)
    down_grads = jnp.stack([down_first, down_second]).astype(jnp.bfloat16)
    return (section_out, input_grads, up_grads, down_grads)
```

```python
import functools
import math

import jax
import jax.numpy as jnp
from jax import lax
from jax.experimental import pallas as pl
from jax.experimental.pallas import tpu as pltpu
from jax.sharding import PartitionSpec as P

gelu_coef = math.sqrt(2.0 / math.pi)
MESH = pl.DeviceIdType.MESH
BF = jnp.bfloat16
F32 = jnp.float32
ROWS = 16
NY = 2

HID, BACK = 0, 1
ACT, DEL = 0, 1
OUT, THR = 0, 1
XS, IS = 0, 1


def gelu_parts(values):
    tangent = jnp.tanh(gelu_coef * (values + 0.044715 * values * values * values))
    half = 0.5 * (1.0 + tangent)
    return values * half, half + 0.5 * values * (1.0 - tangent * tangent) * gelu_coef * (
        1.0 + 3.0 * 0.044715 * values * values
    )


def power_of_two(exponent):
    return jnp.where(
        exponent == -9,
        2.0**-9,
        jnp.where(exponent == -8, 2.0**-8, jnp.where(exponent == -7, 2.0**-7, 2.0**-6)),
    ).astype(F32)


def inverse_power(exponent):
    return jnp.where(
        exponent == -9,
        2.0**9,
        jnp.where(exponent == -8, 2.0**8, jnp.where(exponent == -7, 2.0**7, 2.0**6)),
    ).astype(F32)


def column_step(width):
    return 256 if width % 256 == 0 else 128


def kernel(
    ndp,
    nz,
    x_ref,
    c_ref,
    e_ref,
    wu_hbm,
    wd_hbm,
    so_ref,
    ig_ref,
    xf_hbm,
    if_hbm,
    af_hbm,
    df_hbm,
    wu,
    wd,
    full,
    part,
    ypart,
    zsum,
    zpart,
    shard,
    wide,
    acc,
    opart,
    odp,
    handed,
    w_sem,
    g_send,
    g_recv,
    y_send,
    y_recv,
    z_send,
    z_recv,
    az_send,
    az_recv,
    ay_send,
    ay_recv,
    o_send,
    o_recv,
    h_send,
    out_sem,
):
    sec = lax.axis_index("section")
    p = lax.axis_index("dp")
    q = lax.axis_index("tensor")
    y = q // nz
    z = q % nz
    micro = x_ref.shape[0]
    tokens = ROWS * ndp
    half = wu.shape[2]
    feats = wu.shape[1]
    my_dp = pl.ds(pl.multiple_of(p * ROWS, ROWS), ROWS)
    my_z = pl.ds(pl.multiple_of(z * ROWS, ROWS), ROWS)
    partner = {"tensor": (1 - y) * nz + z}

    def rows(index):
        return pl.ds(pl.multiple_of(index * ROWS, ROWS), ROWS)

    def dp_peer(j):
        return lax.rem(p + j, ndp)

    def z_peer(d):
        return y * nz + lax.rem(z + d, nz)

    def remote(src, dst, send, recv, where):
        pltpu.make_async_remote_copy(
            src_ref=src, dst_ref=dst, send_sem=send, recv_sem=recv, device_id=where, device_id_type=MESH
        ).start()

    def await_bytes(ref, sem):
        pltpu.make_async_copy(ref, ref, sem).wait()

    loads = []
    for h in range(NY):
        loads.append(pltpu.make_async_copy(wu_hbm.at[:, pl.ds(h * half, half)], wu.at[h], w_sem.at[0, h]))
        loads.append(pltpu.make_async_copy(wd_hbm.at[pl.ds(h * half, half)], wd.at[h], w_sem.at[1, h]))
    for load in loads:
        load.start()

    barrier = pltpu.get_barrier_semaphore()

    @pl.loop(1, ndp)
    def _(j):
        pl.semaphore_signal(barrier, inc=1, device_id={"dp": dp_peer(j)}, device_id_type=MESH)

    @pl.loop(0, ndp)
    def _(j):
        pl.semaphore_signal(
            barrier, inc=1, device_id={"section": 1 - sec, "dp": dp_peer(j)}, device_id_type=MESH
        )

    @pl.loop(1, nz)
    def _(d):
        pl.semaphore_signal(barrier, inc=1, device_id={"tensor": z_peer(d)}, device_id_type=MESH)

    pl.semaphore_signal(barrier, inc=1, device_id=partner, device_id_type=MESH)
    pl.semaphore_wait(barrier, 2 * ndp + nz - 1)

    def gather_own(op, m, source):
        @pl.loop(1, ndp)
        def _(j):
            remote(
                source.at[m], full.at[op, m, my_dp], g_send.at[op, m], g_recv.at[op, m], {"dp": dp_peer(j)}
            )

        full[op, m, my_dp, :] = source[m]

    def hand_over(op, m):
        @pl.loop(0, ndp)
        def _(j):
            remote(
                handed.at[op, m],
                full.at[op, m, my_dp],
                h_send.at[op, m],
                g_recv.at[op, m],
                {"section": 1 - sec, "dp": dp_peer(j)},
            )

    def keep_full(op, m):
        dst = (xf_hbm, if_hbm)[op]
        pltpu.make_async_copy(
            full.at[op, m], dst.at[pl.ds(m * tokens, tokens)], out_sem.at[op, m]
        ).start()

    def product(op, m, h, slot):
        step = column_step(half)

        @pl.loop(0, half // step)
        def _(j):
            at = pl.ds(pl.multiple_of(j * step, step), step)
            if op == HID:
                value = jnp.dot(full[XS, m], wu[h, :, at], preferred_element_type=F32)
            else:
                value = lax.dot_general(
                    full[IS, m], wd[h, at, :], (((1,), (1,)), ((), ())), preferred_element_type=F32
                )
            part[op, m, slot, :, at] = value.astype(BF)

    def stage_a(op, m, arrivals):
        source = (XS, IS)[op]
        await_bytes(full.at[source, m, pl.ds(0, arrivals * ROWS)], g_recv.at[source, m])
        product(op, m, 1 - y, 0)

        @pl.loop(0, nz)
        def _(k):
            there = rows(lax.rem(z + ring_order(k), nz))
            remote(
                part.at[op, m, 0, there],
                ypart.at[op, m, there],
                y_send.at[op, m],
                y_recv.at[op, m, k],
                partner,
            )

        product(op, m, y, 1)
        keep_full(source, m)

    def ring_order(k):
        return nz // 2 + (1 - 2 * (k % 2)) * ((k + 1) // 2)

    def stage_b(op, m):
        def summed(k):
            there = rows(lax.rem(z + ring_order(k), nz))
            await_bytes(ypart.at[op, m, there], y_recv.at[op, m, k])
            return there, (
                part[op, m, 1, there, :].astype(F32) + ypart[op, m, there, :].astype(F32)
            ).astype(BF)

        @pl.loop(0, nz - 1)
        def _(k):
            there, value = summed(k)
            zsum[op, m, there, :] = value
            remote(
                zsum.at[op, m, there],
                zpart.at[op, m, my_z],
                z_send.at[op, m],
                z_recv.at[op, m],
                {"tensor": z_peer(ring_order(k))},
            )

        _, own = summed(nz - 1)
        zpart[op, m, my_z, :] = own

    def reduced(op, m):
        await_bytes(zpart.at[op, m, pl.ds(0, ROWS * (nz - 1))], z_recv.at[op, m])
        total = zpart[op, m, pl.ds(0, ROWS), :].astype(F32)
        for k in range(1, nz):
            total = total + zpart[op, m, pl.ds(ROWS * k, ROWS), :].astype(F32)
        return total

    def spread(op, m, value):
        wide[op, m, y, my_z, :] = value
        mine = wide.at[op, m, y, my_z]

        @pl.loop(0, nz - 1)
        def _(k):
            remote(
                mine,
                mine,
                az_send.at[op, m],
                az_recv.at[op, m, z],
                {"tensor": z_peer(ring_order(k))},
            )

        remote(mine, mine, ay_send.at[op, m], ay_recv.at[op, m], partner)

    def stage_d(op, m):
        @pl.loop(0, nz - 1)
        def _(k):
            there = lax.rem(z + ring_order(nz - 2 - k), nz)
            piece = wide.at[op, m, y, rows(there)]
            await_bytes(piece, az_recv.at[op, m, there])
            remote(piece, piece, ay_send.at[op, m], ay_recv.at[op, m], partner)

    def keep_wide(op, m):
        dst = (af_hbm, df_hbm)[op]
        for h in range(NY):
            pltpu.make_async_copy(
                wide.at[op, m, h],
                dst.at[pl.ds(m * tokens, tokens), pl.ds(h * half, half)],
                out_sem.at[2 + op, m],
            ).start()

    def stage_e(op, m):
        def dots(h, finish):
            for j in range(feats // column_step(feats)):
                at = pl.ds(j * column_step(feats), column_step(feats))
                if op == OUT:
                    value = jnp.dot(wide[op, m, h], wd[h, :, at], preferred_element_type=F32)
                else:
                    value = lax.dot_general(
                        wide[op, m, h], wu[h, at, :], (((1,), (1,)), ((), ())), preferred_element_type=F32
                    )
                finish(at, value)

        def first(at, value):
            acc[:, at] = value

        def second(at, value):
            opart[op, m, :, at] = (acc[:, at] + value).astype(BF)

        dots(y, first)
        await_bytes(wide.at[op, m, 1 - y], ay_recv.at[op, m])
        dots(1 - y, second)

        @pl.loop(1, ndp)
        def _(j):
            to = dp_peer(j)
            remote(
                opart.at[op, m, rows(to)],
                odp.at[op, m, my_dp],
                o_send.at[op, m],
                o_recv.at[op, m],
                {"dp": to},
            )

        odp[op, m, my_dp, :] = opart[op, m, my_dp, :]
        keep_wide(op, m)

    def scattered(op, m):
        await_bytes(odp.at[op, m, pl.ds(0, ROWS * (ndp - 1))], o_recv.at[op, m])
        total = odp[op, m, pl.ds(0, ROWS), :].astype(F32)
        for k in range(1, ndp):
            total = total + odp[op, m, pl.ds(ROWS * k, ROWS), :].astype(F32)
        return total

    def finish_out(m):
        value = (full[XS, m, my_dp, :].astype(F32) + scattered(OUT, m)).astype(BF)
        so_ref[m] = value
        return value

    def finish_through(m):
        through = full[IS, m, my_dp, :].astype(F32) + scattered(THR, m)
        ig_ref[m] = through.astype(BF)
        return through

    def restore(m, through):
        for i in range(e_ref.shape[1]):
            for j in range(e_ref.shape[2]):
                tile = through[8 * i : 8 * i + 8, 128 * j : 128 * j + 128]
                exponent = e_ref[m, i, j]
                packed = jnp.clip(tile * inverse_power(exponent), -448.0, 448.0).astype(BF)
                acc[pl.ds(8 * i, 8), pl.ds(128 * j, 128)] = packed.astype(F32) * power_of_two(exponent)
        handed[IS, m] = acc[pl.ds(0, ROWS), :].astype(BF)

    @pl.when(sec == 0)
    def _():
        for m in range(micro):
            gather_own(XS, m, x_ref)
        for load in loads:
            load.wait()

        def forward_c(m):
            hidden = reduced(HID, m)
            shard[HID, m] = hidden
            spread(ACT, m, gelu_parts(hidden)[0].astype(BF))

        def forward_f(m):
            handed[XS, m] = finish_out(m)
            hand_over(XS, m)

        def backward_c(m):
            delta = reduced(BACK, m) * gelu_parts(shard[HID, m])[1]
            spread(DEL, m, delta.astype(BF))

        stage_a(HID, 0, ndp - 1)
        stage_a(HID, 1, ndp - 1)
        stage_b(HID, 0)
        stage_b(HID, 1)
        forward_c(0)
        forward_c(1)
        stage_d(ACT, 0)
        stage_e(OUT, 0)
        stage_d(ACT, 1)
        forward_f(0)
        stage_e(OUT, 1)
        forward_f(1)

        stage_a(BACK, 0, ndp)
        stage_b(BACK, 0)
        backward_c(0)
        stage_a(BACK, 1, ndp)
        stage_d(DEL, 0)
        stage_b(BACK, 1)
        stage_e(THR, 0)
        backward_c(1)
        finish_through(0)
        stage_d(DEL, 1)
        stage_e(THR, 1)
        finish_through(1)

    @pl.when(sec == 1)
    def _():
        for m in range(micro):
            gather_own(IS, m, c_ref)
        for load in loads:
            load.wait()

        def early_c(m):
            shard[BACK, m] = reduced(BACK, m)

        def turn_c(m):
            active, slope = gelu_parts(reduced(HID, m))
            spread(DEL, m, (shard[BACK, m] * slope).astype(BF))
            shard[HID, m] = active

        def turn_f(m):
            restore(m, finish_through(m))
            hand_over(IS, m)

        stage_a(BACK, 0, ndp - 1)
        stage_a(BACK, 1, ndp - 1)
        stage_b(BACK, 0)
        stage_b(BACK, 1)
        early_c(0)
        early_c(1)

        stage_a(HID, 0, ndp)
        stage_b(HID, 0)
        turn_c(0)
        stage_a(HID, 1, ndp)
        stage_d(DEL, 0)
        stage_b(HID, 1)
        stage_e(THR, 0)
        turn_c(1)
        turn_f(0)
        stage_d(DEL, 1)
        stage_e(THR, 1)
        turn_f(1)

        for m in range(micro):
            spread(ACT, m, shard[HID, m].astype(BF))
        for m in range(micro):
            stage_d(ACT, m)
        for m in range(micro):
            stage_e(OUT, m)
        for m in range(micro):
            finish_out(m)

    for m in range(micro):
        for op in range(2):
            await_bytes(part.at[op, m, 0], y_send.at[op, m])
            await_bytes(zsum.at[op, m, pl.ds(0, ROWS * (nz - 1))], z_send.at[op, m])
            await_bytes(wide.at[op, m, 0, pl.ds(0, ROWS * (nz - 1))], az_send.at[op, m])
            await_bytes(wide.at[op, m, 0], ay_send.at[op, m])
            await_bytes(opart.at[op, m, pl.ds(0, ROWS * (ndp - 1))], o_send.at[op, m])
            await_bytes(full.at[op, m], out_sem.at[op, m])
            await_bytes(wide.at[op, m], out_sem.at[2 + op, m])

        @pl.when(sec == 0)
        def _():
            await_bytes(full.at[XS, m, pl.ds(0, ROWS * (ndp - 1))], g_send.at[XS, m])
            await_bytes(full.at[XS, m], h_send.at[XS, m])

        @pl.when(sec == 1)
        def _():
            await_bytes(full.at[IS, m, pl.ds(0, ROWS * (ndp - 1))], g_send.at[IS, m])
            await_bytes(full.at[IS, m], h_send.at[IS, m])


def per_device(ndp, ntensor, inputs, cotangent, scale_exps, up_weight, down_weight):
    nz = ntensor // NY
    micro, own_rows, feats = inputs.shape
    units = up_weight.shape[2]
    half = units // NY
    tokens = own_rows * ndp
    vmem = pl.BlockSpec(memory_space=pltpu.VMEM)
    anywhere = pl.BlockSpec(memory_space=pl.ANY)
    dma = pltpu.SemaphoreType.DMA
    section_out, input_grads, x_full, i_full, active, delta = pl.pallas_call(
        functools.partial(kernel, ndp, nz),
        out_shape=[
            jax.ShapeDtypeStruct(inputs.shape, BF),
            jax.ShapeDtypeStruct(inputs.shape, BF),
            jax.ShapeDtypeStruct((micro * tokens, feats), BF),
            jax.ShapeDtypeStruct((micro * tokens, feats), BF),
            jax.ShapeDtypeStruct((micro * tokens, units), BF),
            jax.ShapeDtypeStruct((micro * tokens, units), BF),
        ],
        in_specs=[vmem, vmem, pl.BlockSpec(memory_space=pltpu.SMEM), anywhere, anywhere],
        out_specs=[vmem, vmem, anywhere, anywhere, anywhere, anywhere],
        scratch_shapes=[
            pltpu.VMEM((NY, feats, half), BF),
            pltpu.VMEM((NY, half, feats), BF),
            pltpu.VMEM((2, micro, tokens, feats), BF),
            pltpu.VMEM((2, micro, 2, tokens, half), BF),
            pltpu.VMEM((2, micro, tokens, half), BF),
            pltpu.VMEM((2, micro, tokens, half), BF),
            pltpu.VMEM((2, micro, nz * ROWS, half), BF),
            pltpu.VMEM((2, micro, ROWS, half), F32),
            pltpu.VMEM((2, micro, NY, tokens, half), BF),
            pltpu.VMEM((tokens, feats), F32),
            pltpu.VMEM((2, micro, tokens, feats), BF),
            pltpu.VMEM((2, micro, tokens, feats), BF),
            pltpu.VMEM((2, micro, ROWS, feats), BF),
            dma((2, NY)),
            dma((2, micro)),
            dma((2, micro)),
            dma((2, micro)),
            dma((2, micro, nz)),
            dma((2, micro)),
            dma((2, micro)),
            dma((2, micro)),
            dma((2, micro, nz)),
            dma((2, micro)),
            dma((2, micro)),
            dma((2, micro)),
            dma((2, micro)),
            dma((2, micro)),
            dma((4, micro)),
        ],
        compiler_params=pltpu.CompilerParams(
            collective_id=0, has_side_effects=True, vmem_limit_bytes=48 * 1024 * 1024
        ),
        name="relay",
    )(inputs, cotangent, scale_exps, up_weight[0], down_weight[0])
    over_tokens = (((0,), (0,)), ((), ()))
    up_grads = lax.dot_general(x_full, delta, over_tokens, preferred_element_type=F32).astype(BF)
    down_grads = lax.dot_general(active, i_full, over_tokens, preferred_element_type=F32).astype(BF)
    return section_out[None], input_grads[None], up_grads[None], down_grads[None]


def solution(mesh):
    in_specs = (
        P(None, "dp", "tensor"),
        P(None, "dp", "tensor"),
        P(None, "dp", "tensor"),
        P("section", "tensor", "dp"),
        P("section", "dp", "tensor"),
    )
    out_specs = (
        P("section", None, "dp", "tensor"),
        P("section", None, "dp", "tensor"),
        P("section", "tensor", "dp"),
        P("section", "dp", "tensor"),
    )
    return jax.shard_map(
        functools.partial(per_device, mesh.shape["dp"], mesh.shape["tensor"]),
        mesh=mesh,
        in_specs=in_specs,
        out_specs=out_specs,
        check_vma=False,
    )
```

```python
import functools
import math

import jax
import jax.numpy as jnp
from jax import lax
from jax.experimental import pallas as pl
from jax.experimental.pallas import tpu as pltpu
from jax.sharding import PartitionSpec as P

gelu_coef = math.sqrt(2.0 / math.pi)
MESH = pl.DeviceIdType.MESH
BF = jnp.bfloat16
F32 = jnp.float32
ROWS = 16
NY = 2

HID, BACK = 0, 1
ACT, DEL = 0, 1
OUT, THR = 0, 1
XS, IS = 0, 1


START = 0
LOCK = ("a0", "a1", "b0", "b1", "c0", "c1", "d0", "d1", "e0", "e1", "f0", "f1")
ORDER0, ORDER1, ORDER2, ORDERB = LOCK, LOCK, LOCK, LOCK[:6]


def gelu_parts(values):
    tangent = jnp.tanh(gelu_coef * (values + 0.044715 * values * values * values))
    half = 0.5 * (1.0 + tangent)
    return values * half, half + 0.5 * values * (1.0 - tangent * tangent) * gelu_coef * (
        1.0 + 3.0 * 0.044715 * values * values
    )


def power_of_two(exponent):
    return jnp.where(
        exponent == -9,
        2.0**-9,
        jnp.where(exponent == -8, 2.0**-8, jnp.where(exponent == -7, 2.0**-7, 2.0**-6)),
    ).astype(F32)


def inverse_power(exponent):
    return jnp.where(
        exponent == -9,
        2.0**9,
        jnp.where(exponent == -8, 2.0**8, jnp.where(exponent == -7, 2.0**7, 2.0**6)),
    ).astype(F32)


def column_step(width):
    return 256 if width % 256 == 0 else 128


def kernel(
    ndp,
    nz,
    x_hbm,
    c_hbm,
    e_hbm,
    wu_hbm,
    wd_hbm,
    so_ref,
    ig_ref,
    ug_ref,
    dg_ref,
    wu,
    wd,
    full,
    part,
    ypart,
    zsum,
    zpart,
    shard,
    wide,
    acc,
    opart,
    odp,
    handed,
    turned,
    e_ref,
    w_sem,
    r_sem,
    e_sem,
    g_send,
    g_recv,
    y_send,
    y_recv,
    z_send,
    z_recv,
    az_send,
    az_recv,
    ay_send,
    ay_recv,
    o_send,
    o_recv,
    h_send,
    start_sem,
):
    sec = lax.axis_index("section")
    p = lax.axis_index("dp")
    q = lax.axis_index("tensor")
    y = q // nz
    z = q % nz
    micro = x_hbm.shape[0]
    tokens = ROWS * ndp
    half = wu.shape[2]
    feats = wu.shape[1]
    my_dp = pl.ds(pl.multiple_of(p * ROWS, ROWS), ROWS)
    my_z = pl.ds(pl.multiple_of(z * ROWS, ROWS), ROWS)
    partner = {"tensor": (1 - y) * nz + z}

    def rows(index):
        return pl.ds(pl.multiple_of(index * ROWS, ROWS), ROWS)

    nx = ndp // NY

    def ring_order(k, n):
        return n // 2 + (1 - 2 * (k % 2)) * ((k + 1) // 2)

    def dp_peer(j):
        across_y = 1 - j // nx
        x = lax.rem(p // NY + ring_order(lax.rem(j, nx), nx), nx)
        return x * NY + lax.rem(p + across_y, NY)

    def z_peer(d):
        return y * nz + lax.rem(z + d, nz)

    def remote(src, dst, send, recv, where):
        pltpu.make_async_remote_copy(
            src_ref=src, dst_ref=dst, send_sem=send, recv_sem=recv, device_id=where, device_id_type=MESH
        ).start()

    def await_bytes(ref, sem):
        pltpu.make_async_copy(ref, ref, sem).wait()

    loads = []
    for h in range(NY):
        loads.append(pltpu.make_async_copy(wu_hbm.at[:, pl.ds(h * half, half)], wu.at[h], w_sem.at[0, h]))
        loads.append(pltpu.make_async_copy(wd_hbm.at[pl.ds(h * half, half)], wd.at[h], w_sem.at[1, h]))
    for load in loads:
        load.start()
    scales = pltpu.make_async_copy(e_hbm, e_ref, e_sem)
    scales.start()

    def own_rows(op):
        source = (x_hbm, c_hbm)[op]
        return [
            pltpu.make_async_copy(source.at[m], full.at[op, m, my_dp], r_sem.at[m]) for m in range(micro)
        ]

    for op in (XS, IS):

        @pl.when(sec == op)
        def _():
            for load in own_rows(op):
                load.start()

    barrier = pltpu.get_barrier_semaphore()

    @pl.loop(0, ndp - 1)
    def _(j):
        pl.semaphore_signal(barrier, inc=1, device_id={"dp": dp_peer(j)}, device_id_type=MESH)

    @pl.loop(0, ndp)
    def _(j):
        pl.semaphore_signal(
            barrier, inc=1, device_id={"section": 1 - sec, "dp": dp_peer(j)}, device_id_type=MESH
        )

    @pl.loop(1, nz)
    def _(d):
        pl.semaphore_signal(barrier, inc=1, device_id={"tensor": z_peer(d)}, device_id_type=MESH)

    pl.semaphore_signal(barrier, inc=1, device_id=partner, device_id_type=MESH)
    pl.semaphore_wait(barrier, 2 * ndp + nz - 1)

    def gather_own(op):
        for m, load in enumerate(own_rows(op)):
            load.wait()
            mine = full.at[op, m, my_dp]

            @pl.loop(0, ndp - 1)
            def _(j):
                remote(mine, mine, g_send.at[op, m], g_recv.at[op, m], {"dp": dp_peer(j)})

    def hand_over(op, m):
        @pl.loop(0, ndp)
        def _(j):
            remote(
                handed.at[op, m],
                full.at[op, m, my_dp],
                h_send.at[op, m],
                g_recv.at[op, m],
                {"section": 1 - sec, "dp": dp_peer(j)},
            )

    def product(op, m, h, slot):
        step = column_step(half)
        for j in range(half // step):
            at = pl.ds(j * step, step)
            if op == HID:
                value = jnp.dot(full[XS, m], wu[h, :, at], preferred_element_type=F32)
            else:
                value = lax.dot_general(
                    full[IS, m], wd[h, at, :], (((1,), (1,)), ((), ())), preferred_element_type=F32
                )
            part[op, m, slot, :, at] = value.astype(BF)

    def stage_a(op, m, arrivals, before_sends=None):
        source = (XS, IS)[op]
        await_bytes(full.at[source, m, pl.ds(0, arrivals * ROWS)], g_recv.at[source, m])
        product(op, m, 1 - y, 0)
        if before_sends is not None:
            before_sends()

        @pl.loop(0, nz)
        def _(k):
            there = rows(lax.rem(z + ring_order(k, nz), nz))
            remote(
                part.at[op, m, 0, there],
                ypart.at[op, m, there],
                y_send.at[op, m],
                y_recv.at[op, m, k],
                partner,
            )

        product(op, m, y, 1)

    def stage_b(op, m, low, high):
        def summed(k):
            there = rows(lax.rem(z + ring_order(k, nz), nz))
            await_bytes(ypart.at[op, m, there], y_recv.at[op, m, k])
            return there, (
                part[op, m, 1, there, :].astype(F32) + ypart[op, m, there, :].astype(F32)
            ).astype(BF)

        @pl.loop(low, min(high, nz - 1))
        def _(k):
            there, value = summed(k)
            zsum[op, m, there, :] = value
            remote(
                zsum.at[op, m, there],
                zpart.at[op, m, k],
                z_send.at[op, m],
                z_recv.at[op, m],
                {"tensor": z_peer(ring_order(k, nz))},
            )

        if high == nz:
            _, own = summed(nz - 1)
            zpart[op, m, nz - 1] = own

    def reduced(op, m):
        await_bytes(zpart.at[op, m, pl.ds(0, nz - 1)], z_recv.at[op, m])
        total = zpart[op, m, nz - 1].astype(F32)
        for k in range(nz - 1):
            total = total + zpart[op, m, k].astype(F32)
        return total

    def spread(op, m, value):
        wide[op, m, y, my_z, :] = value
        mine = wide.at[op, m, y, my_z]

        @pl.loop(0, nz - 1)
        def _(k):
            remote(
                mine,
                mine,
                az_send.at[op, m],
                az_recv.at[op, m, z],
                {"tensor": z_peer(ring_order(k, nz))},
            )

        remote(mine, mine, ay_send.at[op, m], ay_recv.at[op, m], partner)

    def stage_d(op, m, low, high):
        @pl.loop(low, min(high, nz - 1))
        def _(k):
            there = lax.rem(z + ring_order(nz - 2 - k, nz), nz)
            piece = wide.at[op, m, y, rows(there)]
            await_bytes(piece, az_recv.at[op, m, there])
            remote(piece, piece, ay_send.at[op, m], ay_recv.at[op, m], partner)

    def stage_e(op, m):
        def dots(h, finish):
            for j in range(feats // column_step(feats)):
                at = pl.ds(j * column_step(feats), column_step(feats))
                if op == OUT:
                    value = jnp.dot(wide[op, m, h], wd[h, :, at], preferred_element_type=F32)
                else:
                    value = lax.dot_general(
                        wide[op, m, h], wu[h, at, :], (((1,), (1,)), ((), ())), preferred_element_type=F32
                    )
                finish(at, value)

        def first(at, value):
            acc[:, at] = value

        def second(at, value):
            opart[op, m, :, at] = (acc[:, at] + value).astype(BF)

        dots(y, first)
        await_bytes(wide.at[op, m, 1 - y], ay_recv.at[op, m])
        dots(1 - y, second)

        @pl.loop(0, ndp - 1)
        def _(j):
            to = dp_peer(j)
            remote(
                opart.at[op, m, rows(to)],
                odp.at[op, m, my_dp],
                o_send.at[op, m],
                o_recv.at[op, m],
                {"dp": to},
            )

        odp[op, m, my_dp, :] = opart[op, m, my_dp, :]

    def scattered(op, m):
        await_bytes(odp.at[op, m, pl.ds(0, ROWS * (ndp - 1))], o_recv.at[op, m])
        total = odp[op, m, pl.ds(0, ROWS), :].astype(F32)
        for k in range(1, ndp):
            total = total + odp[op, m, pl.ds(ROWS * k, ROWS), :].astype(F32)
        return total

    def finish_out(m):
        value = (full[XS, m, my_dp, :].astype(F32) + scattered(OUT, m)).astype(BF)
        so_ref[m] = value
        return value

    def finish_through(m):
        through = full[IS, m, my_dp, :].astype(F32) + scattered(THR, m)
        ig_ref[m] = through.astype(BF)
        return through

    def restore(m, through):
        for i in range(e_ref.shape[1]):
            for j in range(e_ref.shape[2]):
                tile = through[8 * i : 8 * i + 8, 128 * j : 128 * j + 128]
                exponent = e_ref[m, i, j]
                packed = jnp.clip(tile * inverse_power(exponent), -448.0, 448.0).astype(BF)
                acc[pl.ds(8 * i, 8), pl.ds(128 * j, 128)] = packed.astype(F32) * power_of_two(exponent)
        handed[IS, m] = acc[pl.ds(0, ROWS), :].astype(BF)

    def up_gradient():
        turned[...] = full[XS].reshape(micro * tokens, feats).T
        step = column_step(half)
        for h in range(NY):
            for j in range(half // step):
                right = wide[DEL, :, h, :, pl.ds(j * step, step)].reshape(micro * tokens, step)
                ug_ref[:, pl.ds(h * half + j * step, step)] = jnp.dot(
                    turned[...], right, preferred_element_type=F32
                ).astype(BF)

    def down_gradient():
        step = column_step(half)
        for h in range(NY):
            for j in range(half // step):
                left = wide[ACT, :, h, :, pl.ds(j * step, step)].reshape(micro * tokens, step)
                dg_ref[pl.ds(h * half + j * step, step), :] = lax.dot_general(
                    left,
                    full[IS].reshape(micro * tokens, feats),
                    (((0,), (0,)), ((), ())),
                    preferred_element_type=F32,
                ).astype(BF)

    def run(order, a, b, c, d=None, e=None, f=None):
        for entry in order:
            name, m = entry[0], int(entry[1])
            if name in "bd":
                low, high = entry[2:].split("-") if len(entry) > 2 else (0, nz)
                {"b": b, "d": d}[name](m, min(int(low), nz), min(int(high), nz))
            else:
                {"a": a, "c": c, "e": e, "f": f}[name](m)

    def stages(first, op, wide_op, opart_op):
        return (
            lambda m: stage_a(op, m, ndp if not first else ndp - 1),
            lambda m, low, high: stage_b(op, m, low, high),
            lambda m, low, high: stage_d(wide_op, m, low, high),
            lambda m: stage_e(opart_op, m),
        )

    @pl.when(sec == 0)
    def _():
        gather_own(XS)
        for load in loads:
            load.wait()
        scales.wait()

        def forward_c(m):
            active, slope = gelu_parts(reduced(HID, m))
            spread(ACT, m, active.astype(BF))
            shard[HID, m] = slope

        def forward_f(m):
            handed[XS, m] = finish_out(m)
            hand_over(XS, m)

        def backward_c(m):
            spread(DEL, m, (reduced(BACK, m) * shard[HID, m]).astype(BF))

        def backward_e(m):
            stage_e(THR, m)
            if m == micro - 1:
                up_gradient()

        def start_other(m):
            if m == START:
                pl.semaphore_signal(start_sem, inc=1, device_id={"section": 1}, device_id_type=MESH)
            stage_e(OUT, m)

        a, b, d, _e = stages(True, HID, ACT, OUT)
        run(ORDER0, a, b, forward_c, d, start_other, forward_f)
        a, b_last, d, _e = stages(False, BACK, DEL, THR)

        def b(m, low, high):
            b_last(m, low, high)
            if m == micro - 1 and high == nz:
                down_gradient()

        run(ORDER2, a, b, backward_c, d, backward_e, finish_through)

    @pl.when(sec == 1)
    def _():
        gather_own(IS)
        for load in loads:
            load.wait()
        scales.wait()

        def early_a(m):
            stage_a(BACK, m, ndp - 1, wait_start if m == 0 else None)

        def early_c(m):
            shard[BACK, m] = reduced(BACK, m)

        def turn_c(m):
            active, slope = gelu_parts(reduced(HID, m))
            spread(DEL, m, (shard[BACK, m] * slope).astype(BF))
            shard[HID, m] = active

        def turn_f(m):
            restore(m, finish_through(m))
            hand_over(IS, m)

        def wait_start():
            pl.semaphore_wait(start_sem, 1)

        def late_c(m):
            spread(ACT, m, shard[HID, m].astype(BF))

        a, b, d, e = stages(True, BACK, DEL, THR)
        run(ORDERB, early_a, b, early_c)
        a, b, d, e = stages(False, HID, DEL, THR)
        run(ORDER1, a, b, turn_c, d, e, turn_f)

        late_c(0)
        late_c(1)
        up_gradient()
        for m in range(micro):
            stage_d(ACT, m, 0, nz)
        for m in range(micro):
            stage_e(OUT, m)
        down_gradient()
        for m in range(micro):
            finish_out(m)

    for m in range(micro):
        for op in range(2):
            await_bytes(part.at[op, m, 0], y_send.at[op, m])
            await_bytes(zsum.at[op, m, pl.ds(0, ROWS * (nz - 1))], z_send.at[op, m])
            await_bytes(wide.at[op, m, 0, pl.ds(0, ROWS * (nz - 1))], az_send.at[op, m])
            await_bytes(wide.at[op, m, 0], ay_send.at[op, m])
            await_bytes(opart.at[op, m, pl.ds(0, ROWS * (ndp - 1))], o_send.at[op, m])

        @pl.when(sec == 0)
        def _():
            await_bytes(full.at[XS, m, pl.ds(0, ROWS * (ndp - 1))], g_send.at[XS, m])
            await_bytes(full.at[XS, m], h_send.at[XS, m])

        @pl.when(sec == 1)
        def _():
            await_bytes(full.at[IS, m, pl.ds(0, ROWS * (ndp - 1))], g_send.at[IS, m])
            await_bytes(full.at[IS, m], h_send.at[IS, m])


def flush(*refs):
    arrays = len(refs) // 2
    sems = refs[-1]
    copies = [
        pltpu.make_async_copy(refs[i], refs[arrays + i], sems.at[i]) for i in range(arrays)
    ]
    for copy in copies:
        copy.start()
    for copy in copies:
        copy.wait()


def per_device(ndp, ntensor, inputs, cotangent, scale_exps, up_weight, down_weight):
    nz = ntensor // NY
    micro, own_rows, feats = inputs.shape
    units = up_weight.shape[2]
    half = units // NY
    tokens = own_rows * ndp
    vmem = pl.BlockSpec(memory_space=pltpu.VMEM)
    far = pl.BlockSpec(memory_space=pltpu.HBM)
    dma = pltpu.SemaphoreType.DMA
    results = pl.pallas_call(
        functools.partial(kernel, ndp, nz),
        out_shape=[
            jax.ShapeDtypeStruct(inputs.shape, BF),
            jax.ShapeDtypeStruct(inputs.shape, BF),
            jax.ShapeDtypeStruct((feats, units), BF),
            jax.ShapeDtypeStruct((units, feats), BF),
        ],
        in_specs=[far] * 5,
        out_specs=[vmem] * 4,
        scratch_shapes=[
            pltpu.VMEM((NY, feats, half), BF),
            pltpu.VMEM((NY, half, feats), BF),
            pltpu.VMEM((2, micro, tokens, feats), BF),
            pltpu.VMEM((2, micro, 2, tokens, half), BF),
            pltpu.VMEM((2, micro, tokens, half), BF),
            pltpu.VMEM((2, micro, tokens, half), BF),
            pltpu.VMEM((2, micro, nz, ROWS, half), BF),
            pltpu.VMEM((2, micro, ROWS, half), F32),
            pltpu.VMEM((2, micro, NY, tokens, half), BF),
            pltpu.VMEM((tokens, feats), F32),
            pltpu.VMEM((2, micro, tokens, feats), BF),
            pltpu.VMEM((2, micro, tokens, feats), BF),
            pltpu.VMEM((2, micro, ROWS, feats), BF),
            pltpu.VMEM((feats, micro * tokens), BF),
            pltpu.SMEM(scale_exps.shape, jnp.int32),
            dma((2, NY)),
            dma((micro,)),
            dma,
            dma((2, micro)),
            dma((2, micro)),
            dma((2, micro)),
            dma((2, micro, nz)),
            dma((2, micro)),
            dma((2, micro)),
            dma((2, micro)),
            dma((2, micro, nz)),
            dma((2, micro)),
            dma((2, micro)),
            dma((2, micro)),
            dma((2, micro)),
            dma((2, micro)),
            pltpu.SemaphoreType.REGULAR,
        ],
        compiler_params=pltpu.CompilerParams(
            collective_id=0, has_side_effects=True, vmem_limit_bytes=48 * 1024 * 1024
        ),
        name="relay",
    )(*[pltpu.with_memory_space_constraint(a, pltpu.HBM) for a in (inputs, cotangent, scale_exps, up_weight[0], down_weight[0])])
    section_out, input_grads, up_grads, down_grads = pl.pallas_call(
        flush,
        out_shape=[jax.ShapeDtypeStruct(result.shape, result.dtype) for result in results],
        in_specs=[vmem] * 4,
        out_specs=[pl.BlockSpec(memory_space=pl.ANY)] * 4,
        scratch_shapes=[dma((4,))],
        compiler_params=pltpu.CompilerParams(vmem_limit_bytes=1024 * 1024),
        name="flush",
    )(*[pltpu.with_memory_space_constraint(result, pltpu.VMEM) for result in results])
    return section_out[None], input_grads[None], up_grads[None], down_grads[None]


def solution(mesh):
    in_specs = (
        P(None, "dp", "tensor"),
        P(None, "dp", "tensor"),
        P(None, "dp", "tensor"),
        P("section", "tensor", "dp"),
        P("section", "dp", "tensor"),
    )
    out_specs = (
        P("section", None, "dp", "tensor"),
        P("section", None, "dp", "tensor"),
        P("section", "tensor", "dp"),
        P("section", "dp", "tensor"),
    )
    return jax.shard_map(
        functools.partial(per_device, mesh.shape["dp"], mesh.shape["tensor"]),
        mesh=mesh,
        in_specs=in_specs,
        out_specs=out_specs,
        check_vma=False,
    )
```

```python
import functools
import math

import jax
import jax.numpy as jnp
from jax import lax
from jax.experimental import pallas as pl
from jax.experimental.pallas import tpu as pltpu
from jax.sharding import PartitionSpec as P

gelu_coef = math.sqrt(2.0 / math.pi)
MESH = pl.DeviceIdType.MESH
BF = jnp.bfloat16
F32 = jnp.float32
ROWS = 16
NY = 2

HID, BACK = 0, 1
ACT, DEL = 0, 1
OUT, THR = 0, 1
XS, IS = 0, 1


RELAY_AT = 3
CUTS = 2


def gelu_parts(values):
    tangent = jnp.tanh(gelu_coef * (values + 0.044715 * values * values * values))
    half = 0.5 * (1.0 + tangent)
    return values * half, half + 0.5 * values * (1.0 - tangent * tangent) * gelu_coef * (
        1.0 + 3.0 * 0.044715 * values * values
    )


def power_of_two(exponent):
    return jnp.where(
        exponent == -9,
        2.0**-9,
        jnp.where(exponent == -8, 2.0**-8, jnp.where(exponent == -7, 2.0**-7, 2.0**-6)),
    ).astype(F32)


def inverse_power(exponent):
    return jnp.where(
        exponent == -9,
        2.0**9,
        jnp.where(exponent == -8, 2.0**8, jnp.where(exponent == -7, 2.0**7, 2.0**6)),
    ).astype(F32)


def column_step(width):
    return 256 if width % 256 == 0 else width


def kernel(
    ndp,
    nz,
    x_hbm,
    c_hbm,
    e_hbm,
    wu_hbm,
    wd_hbm,
    so_ref,
    ig_ref,
    ug_ref,
    dg_ref,
    wu,
    wd,
    full,
    part,
    npart,
    ypart,
    zsum,
    zpart,
    shard,
    wide,
    acc,
    opart,
    odp,
    handed,
    turned,
    e_ref,
    w_sem,
    r_sem,
    e_sem,
    g_send,
    g_recv,
    n_send,
    n_recv,
    y_send,
    y_recv,
    z_send,
    z_recv,
    az_send,
    az_recv,
    an_recv,
    ay_send,
    ay_recv,
    o_send,
    o_recv,
    h_send,
    start_sem,
):
    sec = lax.axis_index("section")
    p = lax.axis_index("dp")
    q = lax.axis_index("tensor")
    y = q // nz
    z = q % nz
    micro = x_hbm.shape[0]
    tokens = ROWS * ndp
    half = wu.shape[2]
    cut = half // CUTS
    feats = wu.shape[1]
    my_dp = pl.ds(pl.multiple_of(p * ROWS, ROWS), ROWS)
    my_z = pl.ds(pl.multiple_of(z * ROWS, ROWS), ROWS)
    partner = {"tensor": (1 - y) * nz + z}

    def rows(index):
        return pl.ds(pl.multiple_of(index * ROWS, ROWS), ROWS)

    nx = ndp // NY

    def ring_order(n):
        return sorted(range(n), key=lambda offset: -min(offset, n - offset))

    dp_order = [(dx, dy) for dy in (1, 0) for dx in ring_order(nx)]
    z_order = ring_order(nz)
    near = sorted({1, nz - 1})
    far = [d for d in z_order if d not in near and d != 0]

    def dp_peer(j):
        dx, dy = dp_order[j]
        return lax.rem(p // NY + dx, nx) * NY + lax.rem(p + dy, NY)

    def z_peer(d):
        return y * nz + lax.rem(z + d, nz)

    def remote(src, dst, send, recv, where):
        pltpu.make_async_remote_copy(
            src_ref=src, dst_ref=dst, send_sem=send, recv_sem=recv, device_id=where, device_id_type=MESH
        ).start()

    def await_bytes(ref, sem):
        pltpu.make_async_copy(ref, ref, sem).wait()

    loads = []
    for h in range(NY):
        loads.append(pltpu.make_async_copy(wu_hbm.at[:, pl.ds(h * half, half)], wu.at[h], w_sem.at[0, h]))
        loads.append(pltpu.make_async_copy(wd_hbm.at[pl.ds(h * half, half)], wd.at[h], w_sem.at[1, h]))
    for load in loads:
        load.start()
    scales = pltpu.make_async_copy(e_hbm, e_ref, e_sem)
    scales.start()

    def own_rows(op):
        source = (x_hbm, c_hbm)[op]
        return [
            pltpu.make_async_copy(source.at[m], full.at[op, m, my_dp], r_sem.at[m]) for m in range(micro)
        ]

    for op in (XS, IS):

        @pl.when(sec == op)
        def _():
            for load in own_rows(op):
                load.start()

    barrier = pltpu.get_barrier_semaphore()

    for j in range(ndp):
        pl.semaphore_signal(
            barrier, inc=1, device_id={"section": 1 - sec, "dp": dp_peer(j)}, device_id_type=MESH
        )
    for j in range(ndp - 1):
        pl.semaphore_signal(barrier, inc=1, device_id={"dp": dp_peer(j)}, device_id_type=MESH)
    for d in z_order[:-1]:
        pl.semaphore_signal(barrier, inc=1, device_id={"tensor": z_peer(d)}, device_id_type=MESH)
    pl.semaphore_signal(barrier, inc=1, device_id=partner, device_id_type=MESH)
    pl.semaphore_wait(barrier, 2 * ndp + nz - 1)

    def gather_own(op):
        for m, load in enumerate(own_rows(op)):
            load.wait()
            mine = full.at[op, m, my_dp]

            for j in range(ndp - 1):
                remote(mine, mine, g_send.at[op, m], g_recv.at[op, m], {"dp": dp_peer(j)})

    def hand_over(op, m):
        for j in range(ndp):
            remote(
                handed.at[op, m],
                full.at[op, m, my_dp],
                h_send.at[op, m],
                g_recv.at[op, m],
                {"section": 1 - sec, "dp": dp_peer(j)},
            )

    def product(op, m, h, slot, c):
        step = column_step(cut)
        for j in range(cut // step):
            here = pl.ds(c * cut + j * step, step)
            if op == HID:
                value = jnp.dot(full[XS, m], wu[h, :, here], preferred_element_type=F32)
            else:
                value = lax.dot_general(
                    full[IS, m], wd[h, here, :], (((1,), (1,)), ((), ())), preferred_element_type=F32
                )
            part[op, m, slot, c, :, pl.ds(j * step, step)] = value.astype(BF)

    def there(d):
        return rows(lax.rem(z + d, nz))

    def stage_a(op, m, arrivals, before_sends=None):
        source = (XS, IS)[op]
        await_bytes(full.at[source, m, pl.ds(0, arrivals * ROWS)], g_recv.at[source, m])
        for c in range(CUTS):
            product(op, m, 1 - y, 0, c)
            if before_sends is not None and c == 0:
                before_sends()
            for k, d in enumerate(near):
                remote(
                    part.at[op, m, 0, c, there(d)],
                    npart.at[op, m, c, k],
                    n_send.at[op, m],
                    n_recv.at[op, m, c],
                    {"tensor": z_peer(d)},
                )
            for k, d in enumerate(far):
                remote(
                    part.at[op, m, 0, c, there(d)],
                    ypart.at[op, m, c, there(d)],
                    y_send.at[op, m],
                    y_recv.at[op, m, c, k],
                    partner,
                )
        for c in range(CUTS):
            product(op, m, y, 1, c)
            for k, d in enumerate(near):
                send_z(part.at[op, m, 1, c, there(d)], op, m, c, len(far) + k, d)

    def send_z(source, op, m, c, slot, d):
        remote(
            source,
            zpart.at[op, m, c, slot],
            z_send.at[op, m],
            z_recv.at[op, m, c],
            {"tensor": z_peer(d)},
        )

    def relay_near(op, m, c):
        await_bytes(npart.at[op, m, c], n_recv.at[op, m, c])
        total = part[op, m, 0, c, my_z, :].astype(F32)
        for k in range(len(near)):
            total = total + npart[op, m, c, k].astype(F32)
        zsum[op, m, c, my_z, :] = total.astype(BF)
        remote(
            zsum.at[op, m, c, my_z],
            ypart.at[op, m, c, my_z],
            y_send.at[op, m],
            y_recv.at[op, m, c, len(far)],
            partner,
        )

    def with_partner(op, m, c, k, d):
        piece = there(d)
        await_bytes(ypart.at[op, m, c, piece], y_recv.at[op, m, c, k])
        return part[op, m, 1, c, piece, :].astype(F32) + ypart[op, m, c, piece, :].astype(F32)

    def stage_b(op, m, c):
        for k, d in enumerate(far):
            if k == RELAY_AT:
                relay_near(op, m, c)
            zsum[op, m, c, there(d), :] = with_partner(op, m, c, k, d).astype(BF)
            send_z(zsum.at[op, m, c, there(d)], op, m, c, k, d)
        if RELAY_AT >= len(far):
            relay_near(op, m, c)

    def reduced(op, m, c):
        total = with_partner(op, m, c, len(far), 0)
        await_bytes(zpart.at[op, m, c], z_recv.at[op, m, c])
        for k in range(nz - 1):
            total = total + zpart[op, m, c, k].astype(F32)
        return total

    def spread(op, m, c, value):
        wide[op, m, y, c, my_z, :] = value
        mine = wide.at[op, m, y, c, my_z]
        for d in z_order[:-1]:
            remote(
                mine,
                mine,
                az_send.at[op, m],
                az_recv.at[op, m, c, z],
                {"tensor": z_peer(d)},
            )
        remote(mine, mine, ay_send.at[op, m], an_recv.at[op, m, c], partner)

    def stage_d(op, m, c):
        def arrived(d):
            piece = wide.at[op, m, y, c, there(d)]
            await_bytes(piece, az_recv.at[op, m, c, lax.rem(z + d, nz)])
            return piece

        opposite = wide.at[op, m, 1 - y, c, my_z]
        await_bytes(opposite, an_recv.at[op, m, c])
        for d in near:
            remote(opposite, opposite, ay_send.at[op, m], ay_recv.at[op, m], {"tensor": z_peer(d)})
        for d in far[::-1]:
            piece = arrived(d)
            remote(piece, piece, ay_send.at[op, m], ay_recv.at[op, m], partner)
        for d in near:
            arrived(d)

    def stage_e(op, m):
        def dots(h, finish):
            step = column_step(feats)
            for j in range(feats // step):
                at = pl.ds(j * step, step)
                value = None
                for c in range(CUTS):
                    here = pl.ds(c * cut, cut)
                    if op == OUT:
                        term = jnp.dot(wide[op, m, h, c], wd[h, here, at], preferred_element_type=F32)
                    else:
                        term = lax.dot_general(
                            wide[op, m, h, c],
                            wu[h, at, here],
                            (((1,), (1,)), ((), ())),
                            preferred_element_type=F32,
                        )
                    value = term if value is None else value + term
                finish(at, value)

        def first(at, value):
            acc[:, at] = value

        def second(at, value):
            opart[op, m, :, at] = (acc[:, at] + value).astype(BF)

        dots(y, first)
        await_bytes(wide.at[op, m, 1 - y, :, pl.ds(0, ROWS * (nz - 1))], ay_recv.at[op, m])
        dots(1 - y, second)

        for j in range(ndp - 1):
            to = dp_peer(j)
            remote(
                opart.at[op, m, rows(to)],
                odp.at[op, m, my_dp],
                o_send.at[op, m],
                o_recv.at[op, m],
                {"dp": to},
            )

        odp[op, m, my_dp, :] = opart[op, m, my_dp, :]

    def scattered(op, m):
        await_bytes(odp.at[op, m, pl.ds(0, ROWS * (ndp - 1))], o_recv.at[op, m])
        total = odp[op, m, pl.ds(0, ROWS), :].astype(F32)
        for k in range(1, ndp):
            total = total + odp[op, m, pl.ds(ROWS * k, ROWS), :].astype(F32)
        return total

    def finish_out(m):
        value = (full[XS, m, my_dp, :].astype(F32) + scattered(OUT, m)).astype(BF)
        so_ref[m] = value
        return value

    def finish_through(m):
        through = full[IS, m, my_dp, :].astype(F32) + scattered(THR, m)
        ig_ref[m] = through.astype(BF)
        return through

    def restore(m, through):
        for i in range(e_ref.shape[1]):
            for j in range(e_ref.shape[2]):
                tile = through[8 * i : 8 * i + 8, 128 * j : 128 * j + 128]
                exponent = e_ref[m, i, j]
                packed = jnp.clip(tile * inverse_power(exponent), -448.0, 448.0).astype(BF)
                acc[pl.ds(8 * i, 8), pl.ds(128 * j, 128)] = packed.astype(F32) * power_of_two(exponent)
        handed[IS, m] = acc[pl.ds(0, ROWS), :].astype(BF)

    def up_gradient():
        turned[...] = full[XS].reshape(micro * tokens, feats).T
        step = column_step(cut)
        for h in range(NY):
            for c in range(CUTS):
                for j in range(cut // step):
                    right = wide[DEL, :, h, c, :, pl.ds(j * step, step)].reshape(micro * tokens, step)
                    ug_ref[:, pl.ds(h * half + c * cut + j * step, step)] = jnp.dot(
                        turned[...], right, preferred_element_type=F32
                    ).astype(BF)

    def down_gradient():
        step = column_step(cut)
        for h in range(NY):
            for c in range(CUTS):
                for j in range(cut // step):
                    left = wide[ACT, :, h, c, :, pl.ds(j * step, step)].reshape(micro * tokens, step)
                    dg_ref[pl.ds(h * half + c * cut + j * step, step), :] = lax.dot_general(
                        left,
                        full[IS].reshape(micro * tokens, feats),
                        (((0,), (0,)), ((), ())),
                        preferred_element_type=F32,
                    ).astype(BF)

    def all_of(stage, *args):
        for m in range(micro):
            stage(*args, m)

    def all_cuts(stage, *args):
        for m in range(micro):
            for c in range(CUTS):
                stage(*args, m, c)

    def strip(c):
        return pl.ds(c * cut, cut)

    @pl.when(sec == 0)
    def _():
        gather_own(XS)
        for load in loads:
            load.wait()
        scales.wait()

        def forward_c(m, c):
            active, slope = gelu_parts(reduced(HID, m, c))
            spread(ACT, m, c, active.astype(BF))
            shard[HID, m, :, strip(c)] = slope

        def forward_f(m):
            handed[XS, m] = finish_out(m)
            hand_over(XS, m)

        def backward_c(m, c):
            spread(DEL, m, c, (reduced(BACK, m, c) * shard[HID, m, :, strip(c)]).astype(BF))

        for m in range(micro):
            stage_a(HID, m, ndp - 1)
        all_cuts(stage_b, HID)
        all_cuts(forward_c)
        all_cuts(stage_d, ACT)
        pl.semaphore_signal(start_sem, inc=1, device_id={"section": 1}, device_id_type=MESH)
        all_of(stage_e, OUT)
        all_of(forward_f)

        for m in range(micro):
            stage_a(BACK, m, ndp)
        all_cuts(stage_b, BACK)
        down_gradient()
        all_cuts(backward_c)
        all_cuts(stage_d, DEL)
        all_of(stage_e, THR)
        up_gradient()
        all_of(finish_through)

    @pl.when(sec == 1)
    def _():
        gather_own(IS)
        for load in loads:
            load.wait()
        scales.wait()

        def wait_start():
            pl.semaphore_wait(start_sem, 1)

        def early_c(m, c):
            shard[BACK, m, :, strip(c)] = reduced(BACK, m, c)

        def turn_c(m, c):
            active, slope = gelu_parts(reduced(HID, m, c))
            spread(DEL, m, c, (shard[BACK, m, :, strip(c)] * slope).astype(BF))
            shard[HID, m, :, strip(c)] = active

        def turn_f(m):
            restore(m, finish_through(m))
            hand_over(IS, m)

        def late_c(m, c):
            spread(ACT, m, c, shard[HID, m, :, strip(c)].astype(BF))

        for m in range(micro):
            stage_a(BACK, m, ndp - 1, wait_start if m == 0 else None)
        all_cuts(stage_b, BACK)
        all_cuts(early_c)

        for m in range(micro):
            stage_a(HID, m, ndp)
        all_cuts(stage_b, HID)
        all_cuts(turn_c)
        all_cuts(stage_d, DEL)
        all_of(stage_e, THR)
        all_of(turn_f)

        for m in range(micro):
            for c in range(CUTS):
                late_c(m, c)
                if m == 0 and c == 0:
                    up_gradient()
                stage_d(ACT, m, c)
        all_of(stage_e, OUT)
        down_gradient()
        all_of(finish_out)

    for m in range(micro):
        for op in range(2):
            await_bytes(part.at[op, m, 0, :, pl.ds(0, ROWS * (len(far) + 1))], y_send.at[op, m])
            await_bytes(part.at[op, m, 0, :, pl.ds(0, ROWS * len(near))], n_send.at[op, m])
            await_bytes(zsum.at[op, m, :, pl.ds(0, ROWS * (nz - 1))], z_send.at[op, m])
            await_bytes(wide.at[op, m, 0, :, pl.ds(0, ROWS * (nz - 1))], az_send.at[op, m])
            await_bytes(wide.at[op, m, 0], ay_send.at[op, m])
            await_bytes(opart.at[op, m, pl.ds(0, ROWS * (ndp - 1))], o_send.at[op, m])

        @pl.when(sec == 0)
        def _():
            await_bytes(full.at[XS, m, pl.ds(0, ROWS * (ndp - 1))], g_send.at[XS, m])
            await_bytes(full.at[XS, m], h_send.at[XS, m])

        @pl.when(sec == 1)
        def _():
            await_bytes(full.at[IS, m, pl.ds(0, ROWS * (ndp - 1))], g_send.at[IS, m])
            await_bytes(full.at[IS, m], h_send.at[IS, m])


def flush(*refs):
    arrays = len(refs) // 2
    sems = refs[-1]
    copies = [
        pltpu.make_async_copy(refs[i], refs[arrays + i], sems.at[i]) for i in range(arrays)
    ]
    for copy in copies:
        copy.start()
    for copy in copies:
        copy.wait()


def per_device(ndp, ntensor, inputs, cotangent, scale_exps, up_weight, down_weight):
    nz = ntensor // NY
    micro, own_rows, feats = inputs.shape
    units = up_weight.shape[2]
    half = units // NY
    cut = half // CUTS
    tokens = own_rows * ndp
    vmem = pl.BlockSpec(memory_space=pltpu.VMEM)
    far = pl.BlockSpec(memory_space=pltpu.HBM)
    dma = pltpu.SemaphoreType.DMA
    results = pl.pallas_call(
        functools.partial(kernel, ndp, nz),
        out_shape=[
            jax.ShapeDtypeStruct(inputs.shape, BF),
            jax.ShapeDtypeStruct(inputs.shape, BF),
            jax.ShapeDtypeStruct((feats, units), BF),
            jax.ShapeDtypeStruct((units, feats), BF),
        ],
        in_specs=[far] * 5,
        out_specs=[vmem] * 4,
        scratch_shapes=[
            pltpu.VMEM((NY, feats, half), BF),
            pltpu.VMEM((NY, half, feats), BF),
            pltpu.VMEM((2, micro, tokens, feats), BF),
            pltpu.VMEM((2, micro, 2, CUTS, tokens, cut), BF),
            pltpu.VMEM((2, micro, CUTS, len({1, nz - 1}), ROWS, cut), BF),
            pltpu.VMEM((2, micro, CUTS, tokens, cut), BF),
            pltpu.VMEM((2, micro, CUTS, tokens, cut), BF),
            pltpu.VMEM((2, micro, CUTS, nz - 1, ROWS, cut), BF),
            pltpu.VMEM((2, micro, ROWS, half), F32),
            pltpu.VMEM((2, micro, NY, CUTS, tokens, cut), BF),
            pltpu.VMEM((tokens, feats), F32),
            pltpu.VMEM((2, micro, tokens, feats), BF),
            pltpu.VMEM((2, micro, tokens, feats), BF),
            pltpu.VMEM((2, micro, ROWS, feats), BF),
            pltpu.VMEM((feats, micro * tokens), BF),
            pltpu.SMEM(scale_exps.shape, jnp.int32),
            dma((2, NY)),
            dma((micro,)),
            dma,
            dma((2, micro)),
            dma((2, micro)),
            dma((2, micro)),
            dma((2, micro, CUTS)),
            dma((2, micro)),
            dma((2, micro, CUTS, nz)),
            dma((2, micro)),
            dma((2, micro, CUTS)),
            dma((2, micro)),
            dma((2, micro, CUTS, nz)),
            dma((2, micro, CUTS)),
            dma((2, micro)),
            dma((2, micro)),
            dma((2, micro)),
            dma((2, micro)),
            dma((2, micro)),
            pltpu.SemaphoreType.REGULAR,
        ],
        compiler_params=pltpu.CompilerParams(
            collective_id=0, has_side_effects=True, vmem_limit_bytes=48 * 1024 * 1024
        ),
        name="relay",
    )(*[pltpu.with_memory_space_constraint(a, pltpu.HBM) for a in (inputs, cotangent, scale_exps, up_weight[0], down_weight[0])])
    section_out, input_grads, up_grads, down_grads = pl.pallas_call(
        flush,
        out_shape=[jax.ShapeDtypeStruct(result.shape, result.dtype) for result in results],
        in_specs=[vmem] * 4,
        out_specs=[pl.BlockSpec(memory_space=pl.ANY)] * 4,
        scratch_shapes=[dma((4,))],
        compiler_params=pltpu.CompilerParams(vmem_limit_bytes=1024 * 1024),
        name="flush",
    )(*[pltpu.with_memory_space_constraint(result, pltpu.VMEM) for result in results])
    return section_out[None], input_grads[None], up_grads[None], down_grads[None]


def solution(mesh):
    in_specs = (
        P(None, "dp", "tensor"),
        P(None, "dp", "tensor"),
        P(None, "dp", "tensor"),
        P("section", "tensor", "dp"),
        P("section", "dp", "tensor"),
    )
    out_specs = (
        P("section", None, "dp", "tensor"),
        P("section", None, "dp", "tensor"),
        P("section", "tensor", "dp"),
        P("section", "dp", "tensor"),
    )
    return jax.shard_map(
        functools.partial(per_device, mesh.shape["dp"], mesh.shape["tensor"]),
        mesh=mesh,
        in_specs=in_specs,
        out_specs=out_specs,
        check_vma=False,
    )
```

```python
import functools
import math

import jax
import jax.numpy as jnp
from jax import lax
from jax.experimental import pallas as pl
from jax.experimental.pallas import tpu as pltpu
from jax.sharding import PartitionSpec as P

gelu_coef = math.sqrt(2.0 / math.pi)
MESH = pl.DeviceIdType.MESH
BF = jnp.bfloat16
F32 = jnp.float32
ROWS = 16
NY = 2

HID, BACK = 0, 1
ACT, DEL = 0, 1
OUT, THR = 0, 1
XS, IS = 0, 1


RELAY_AT = 3
CUTS = 2


def gelu_parts(values):
    tangent = jnp.tanh(gelu_coef * (values + 0.044715 * values * values * values))
    half = 0.5 * (1.0 + tangent)
    return values * half, half + 0.5 * values * (1.0 - tangent * tangent) * gelu_coef * (
        1.0 + 3.0 * 0.044715 * values * values
    )


def power_of_two(exponent):
    return jnp.where(
        exponent == -9,
        2.0**-9,
        jnp.where(exponent == -8, 2.0**-8, jnp.where(exponent == -7, 2.0**-7, 2.0**-6)),
    ).astype(F32)


def inverse_power(exponent):
    return jnp.where(
        exponent == -9,
        2.0**9,
        jnp.where(exponent == -8, 2.0**8, jnp.where(exponent == -7, 2.0**7, 2.0**6)),
    ).astype(F32)


def column_step(width):
    return 256 if width % 256 == 0 else width


def kernel(
    ndp,
    nz,
    x_hbm,
    c_hbm,
    e_hbm,
    wu_hbm,
    wd_hbm,
    so_ref,
    ig_ref,
    ug_ref,
    dg_ref,
    wu,
    wd,
    full,
    part,
    npart,
    ypart,
    zsum,
    zpart,
    shard,
    wide,
    acc,
    opart,
    odp,
    handed,
    turned,
    e_ref,
    w_sem,
    r_sem,
    e_sem,
    g_send,
    g_recv,
    n_send,
    n_recv,
    y_send,
    y_recv,
    z_send,
    z_recv,
    az_send,
    az_recv,
    an_recv,
    ay_send,
    ay_recv,
    o_send,
    o_recv,
    h_send,
    start_sem,
):
    sec = lax.axis_index("section")
    p = lax.axis_index("dp")
    q = lax.axis_index("tensor")
    y = q // nz
    z = q % nz
    micro = x_hbm.shape[0]
    tokens = ROWS * ndp
    half = wu.shape[2]
    cut = half // CUTS
    feats = wu.shape[1]
    my_dp = pl.ds(pl.multiple_of(p * ROWS, ROWS), ROWS)
    my_z = pl.ds(pl.multiple_of(z * ROWS, ROWS), ROWS)
    partner = {"tensor": (1 - y) * nz + z}

    def rows(index):
        return pl.ds(pl.multiple_of(index * ROWS, ROWS), ROWS)

    nx = ndp // NY

    def ring_order(n):
        return sorted(range(n), key=lambda offset: -min(offset, n - offset))

    dp_order = [(dx, dy) for dy in (1, 0) for dx in ring_order(nx)]
    z_order = ring_order(nz)
    near = sorted({1, nz - 1})
    far = [d for d in z_order if d not in near and d != 0]

    def dp_peer(j):
        dx, dy = dp_order[j]
        return lax.rem(p // NY + dx, nx) * NY + lax.rem(p + dy, NY)

    def z_peer(d):
        return y * nz + lax.rem(z + d, nz)

    def remote(src, dst, send, recv, where):
        pltpu.make_async_remote_copy(
            src_ref=src, dst_ref=dst, send_sem=send, recv_sem=recv, device_id=where, device_id_type=MESH
        ).start()

    def await_bytes(ref, sem):
        pltpu.make_async_copy(ref, ref, sem).wait()

    loads = []
    for h in range(NY):
        loads.append(pltpu.make_async_copy(wu_hbm.at[:, pl.ds(h * half, half)], wu.at[h], w_sem.at[0, h]))
        loads.append(pltpu.make_async_copy(wd_hbm.at[pl.ds(h * half, half)], wd.at[h], w_sem.at[1, h]))
    for load in loads:
        load.start()
    scales = pltpu.make_async_copy(e_hbm, e_ref, e_sem)
    scales.start()

    def own_rows(op):
        source = (x_hbm, c_hbm)[op]
        return [
            pltpu.make_async_copy(source.at[m], full.at[op, m, my_dp], r_sem.at[m]) for m in range(micro)
        ]

    for op in (XS, IS):

        @pl.when(sec == op)
        def _():
            for load in own_rows(op):
                load.start()

    barrier = pltpu.get_barrier_semaphore()

    for j in range(ndp):
        pl.semaphore_signal(
            barrier, inc=1, device_id={"section": 1 - sec, "dp": dp_peer(j)}, device_id_type=MESH
        )
    for j in range(ndp - 1):
        pl.semaphore_signal(barrier, inc=1, device_id={"dp": dp_peer(j)}, device_id_type=MESH)
    for d in z_order[:-1]:
        pl.semaphore_signal(barrier, inc=1, device_id={"tensor": z_peer(d)}, device_id_type=MESH)
    pl.semaphore_signal(barrier, inc=1, device_id=partner, device_id_type=MESH)
    pl.semaphore_wait(barrier, 2 * ndp + nz - 1)

    def gather_own(op):
        for m, load in enumerate(own_rows(op)):
            load.wait()
            mine = full.at[op, m, my_dp]

            for j in range(ndp - 1):
                remote(mine, mine, g_send.at[op, m], g_recv.at[op, m], {"dp": dp_peer(j)})

    def hand_over(op, m):
        for j in range(ndp):
            remote(
                handed.at[op, m],
                full.at[op, m, my_dp],
                h_send.at[op, m],
                g_recv.at[op, m],
                {"section": 1 - sec, "dp": dp_peer(j)},
            )

    def product(op, m, h, slot, c):
        step = column_step(cut)
        for j in range(cut // step):
            here = pl.ds(c * cut + j * step, step)
            if op == HID:
                value = jnp.dot(full[XS, m], wu[h, :, here], preferred_element_type=F32)
            else:
                value = lax.dot_general(
                    full[IS, m], wd[h, here, :], (((1,), (1,)), ((), ())), preferred_element_type=F32
                )
            part[op, m, slot, c, :, pl.ds(j * step, step)] = value.astype(BF)

    def there(d):
        return rows(lax.rem(z + d, nz))

    def stage_a(op, m, arrivals, before_sends=None):
        source = (XS, IS)[op]
        await_bytes(full.at[source, m, pl.ds(0, arrivals * ROWS)], g_recv.at[source, m])
        for c in range(CUTS):
            product(op, m, 1 - y, 0, c)
            if before_sends is not None and c == 0:
                before_sends()
            for k, d in enumerate(near):
                remote(
                    part.at[op, m, 0, c, there(d)],
                    npart.at[op, m, c, k],
                    n_send.at[op, m],
                    n_recv.at[op, m, c],
                    {"tensor": z_peer(d)},
                )
            for k, d in enumerate(far):
                remote(
                    part.at[op, m, 0, c, there(d)],
                    ypart.at[op, m, c, there(d)],
                    y_send.at[op, m],
                    y_recv.at[op, m, c, k],
                    partner,
                )
        for c in range(CUTS):
            product(op, m, y, 1, c)
            for k, d in enumerate(near):
                send_z(part.at[op, m, 1, c, there(d)], op, m, c, len(far) + k, d)

    def send_z(source, op, m, c, slot, d):
        remote(
            source,
            zpart.at[op, m, c, slot],
            z_send.at[op, m],
            z_recv.at[op, m, c],
            {"tensor": z_peer(d)},
        )

    def relay_near(op, m, c):
        await_bytes(npart.at[op, m, c], n_recv.at[op, m, c])
        total = part[op, m, 0, c, my_z, :].astype(F32)
        for k in range(len(near)):
            total = total + npart[op, m, c, k].astype(F32)
        zsum[op, m, c, my_z, :] = total.astype(BF)
        remote(
            zsum.at[op, m, c, my_z],
            ypart.at[op, m, c, my_z],
            y_send.at[op, m],
            y_recv.at[op, m, c, len(far)],
            partner,
        )

    def with_partner(op, m, c, k, d):
        piece = there(d)
        await_bytes(ypart.at[op, m, c, piece], y_recv.at[op, m, c, k])
        return part[op, m, 1, c, piece, :].astype(F32) + ypart[op, m, c, piece, :].astype(F32)

    def stage_b(op, m, c):
        for k, d in enumerate(far):
            if k == RELAY_AT:
                relay_near(op, m, c)
            zsum[op, m, c, there(d), :] = with_partner(op, m, c, k, d).astype(BF)
            send_z(zsum.at[op, m, c, there(d)], op, m, c, k, d)
        if RELAY_AT >= len(far):
            relay_near(op, m, c)

    def reduced(op, m, c):
        total = with_partner(op, m, c, len(far), 0)
        await_bytes(zpart.at[op, m, c], z_recv.at[op, m, c])
        for k in range(nz - 1):
            total = total + zpart[op, m, c, k].astype(F32)
        return total

    def spread(op, m, c, value):
        wide[op, m, y, c, my_z, :] = value
        mine = wide.at[op, m, y, c, my_z]
        for d in z_order[:-1]:
            remote(
                mine,
                mine,
                az_send.at[op, m],
                az_recv.at[op, m, c, z],
                {"tensor": z_peer(d)},
            )
        remote(mine, mine, ay_send.at[op, m], an_recv.at[op, m, c], partner)

    def stage_d(op, m, c):
        def arrived(d):
            piece = wide.at[op, m, y, c, there(d)]
            await_bytes(piece, az_recv.at[op, m, c, lax.rem(z + d, nz)])
            return piece

        opposite = wide.at[op, m, 1 - y, c, my_z]
        await_bytes(opposite, an_recv.at[op, m, c])
        for d in near:
            remote(opposite, opposite, ay_send.at[op, m], ay_recv.at[op, m], {"tensor": z_peer(d)})
        for d in far[::-1]:
            piece = arrived(d)
            remote(piece, piece, ay_send.at[op, m], ay_recv.at[op, m], partner)
        for d in near:
            arrived(d)

    def stage_e(op, m):
        def dots(h, finish):
            step = column_step(feats)
            for j in range(feats // step):
                at = pl.ds(j * step, step)
                value = None
                for c in range(CUTS):
                    here = pl.ds(c * cut, cut)
                    if op == OUT:
                        term = jnp.dot(wide[op, m, h, c], wd[h, here, at], preferred_element_type=F32)
                    else:
                        term = lax.dot_general(
                            wide[op, m, h, c],
                            wu[h, at, here],
                            (((1,), (1,)), ((), ())),
                            preferred_element_type=F32,
                        )
                    value = term if value is None else value + term
                finish(at, value)

        def first(at, value):
            acc[:, at] = value

        def second(at, value):
            opart[op, m, :, at] = (acc[:, at] + value).astype(BF)

        dots(y, first)
        await_bytes(wide.at[op, m, 1 - y, :, pl.ds(0, ROWS * (nz - 1))], ay_recv.at[op, m])
        dots(1 - y, second)

        for j in range(ndp - 1):
            to = dp_peer(j)
            remote(
                opart.at[op, m, rows(to)],
                odp.at[op, m, my_dp],
                o_send.at[op, m],
                o_recv.at[op, m],
                {"dp": to},
            )

        odp[op, m, my_dp, :] = opart[op, m, my_dp, :]

    def scattered(op, m):
        await_bytes(odp.at[op, m, pl.ds(0, ROWS * (ndp - 1))], o_recv.at[op, m])
        total = odp[op, m, pl.ds(0, ROWS), :].astype(F32)
        for k in range(1, ndp):
            total = total + odp[op, m, pl.ds(ROWS * k, ROWS), :].astype(F32)
        return total

    def finish_out(m):
        value = (full[XS, m, my_dp, :].astype(F32) + scattered(OUT, m)).astype(BF)
        so_ref[m] = value
        return value

    def finish_through(m):
        through = full[IS, m, my_dp, :].astype(F32) + scattered(THR, m)
        ig_ref[m] = through.astype(BF)
        return through

    def restore(m, through):
        for i in range(e_ref.shape[1]):
            for j in range(e_ref.shape[2]):
                tile = through[8 * i : 8 * i + 8, 128 * j : 128 * j + 128]
                exponent = e_ref[m, i, j]
                packed = jnp.clip(tile * inverse_power(exponent), -448.0, 448.0).astype(BF)
                acc[pl.ds(8 * i, 8), pl.ds(128 * j, 128)] = packed.astype(F32) * power_of_two(exponent)
        handed[IS, m] = acc[pl.ds(0, ROWS), :].astype(BF)

    def up_gradient():
        turned[...] = full[XS].reshape(micro * tokens, feats).T
        step = column_step(cut)
        for h in range(NY):
            for c in range(CUTS):
                for j in range(cut // step):
                    right = wide[DEL, :, h, c, :, pl.ds(j * step, step)].reshape(micro * tokens, step)
                    ug_ref[:, pl.ds(h * half + c * cut + j * step, step)] = jnp.dot(
                        turned[...], right, preferred_element_type=F32
                    ).astype(BF)

    def down_gradient():
        step = column_step(cut)
        for h in range(NY):
            for c in range(CUTS):
                for j in range(cut // step):
                    left = wide[ACT, :, h, c, :, pl.ds(j * step, step)].reshape(micro * tokens, step)
                    dg_ref[pl.ds(h * half + c * cut + j * step, step), :] = lax.dot_general(
                        left,
                        full[IS].reshape(micro * tokens, feats),
                        (((0,), (0,)), ((), ())),
                        preferred_element_type=F32,
                    ).astype(BF)

    def all_of(stage, *args):
        for m in range(micro):
            stage(*args, m)

    def all_cuts(stage, *args):
        for m in range(micro):
            for c in range(CUTS):
                stage(*args, m, c)

    def strip(c):
        return pl.ds(c * cut, cut)

    @pl.when(sec == 0)
    def _():
        gather_own(XS)
        for load in loads:
            load.wait()
        scales.wait()

        def forward_c(m, c):
            active, slope = gelu_parts(reduced(HID, m, c))
            spread(ACT, m, c, active.astype(BF))
            shard[HID, m, :, strip(c)] = slope

        def forward_f(m):
            handed[XS, m] = finish_out(m)
            hand_over(XS, m)

        def backward_c(m, c):
            spread(DEL, m, c, (reduced(BACK, m, c) * shard[HID, m, :, strip(c)]).astype(BF))

        for m in range(micro):
            stage_a(HID, m, ndp - 1)
        all_cuts(stage_b, HID)
        all_cuts(forward_c)
        all_cuts(stage_d, ACT)
        pl.semaphore_signal(start_sem, inc=1, device_id={"section": 1}, device_id_type=MESH)
        all_of(stage_e, OUT)
        all_of(forward_f)

        for m in range(micro):
            stage_a(BACK, m, ndp)
        all_cuts(stage_b, BACK)
        pl.semaphore_signal(start_sem, inc=1, device_id={"section": 1}, device_id_type=MESH)
        down_gradient()
        all_cuts(backward_c)
        all_cuts(stage_d, DEL)
        all_of(stage_e, THR)
        up_gradient()
        all_of(finish_through)

    @pl.when(sec == 1)
    def _():
        gather_own(IS)
        for load in loads:
            load.wait()
        scales.wait()

        def wait_start():
            pl.semaphore_wait(start_sem, 1)

        def early_c(m, c):
            shard[BACK, m, :, strip(c)] = reduced(BACK, m, c)

        def turn_c(m, c):
            active, slope = gelu_parts(reduced(HID, m, c))
            spread(DEL, m, c, (shard[BACK, m, :, strip(c)] * slope).astype(BF))
            shard[HID, m, :, strip(c)] = active

        def turn_f(m):
            restore(m, finish_through(m))
            hand_over(IS, m)

        def late_c(m, c):
            spread(ACT, m, c, shard[HID, m, :, strip(c)].astype(BF))

        for m in range(micro):
            stage_a(BACK, m, ndp - 1, wait_start if m == 0 else None)
        all_cuts(stage_b, BACK)
        all_cuts(early_c)

        for m in range(micro):
            stage_a(HID, m, ndp)
        all_cuts(stage_b, HID)
        all_cuts(turn_c)
        all_cuts(stage_d, DEL)
        all_cuts(late_c)
        all_of(stage_e, THR)
        all_of(turn_f)

        up_gradient()
        for m in range(micro):
            if m == micro - 1:
                wait_start()
            for c in range(CUTS):
                stage_d(ACT, m, c)
        all_of(stage_e, OUT)
        down_gradient()
        all_of(finish_out)

    for m in range(micro):
        for op in range(2):
            await_bytes(part.at[op, m, 0, :, pl.ds(0, ROWS * (len(far) + 1))], y_send.at[op, m])
            await_bytes(part.at[op, m, 0, :, pl.ds(0, ROWS * len(near))], n_send.at[op, m])
            await_bytes(zsum.at[op, m, :, pl.ds(0, ROWS * (nz - 1))], z_send.at[op, m])
            await_bytes(wide.at[op, m, 0, :, pl.ds(0, ROWS * (nz - 1))], az_send.at[op, m])
            await_bytes(wide.at[op, m, 0], ay_send.at[op, m])
            await_bytes(opart.at[op, m, pl.ds(0, ROWS * (ndp - 1))], o_send.at[op, m])

        @pl.when(sec == 0)
        def _():
            await_bytes(full.at[XS, m, pl.ds(0, ROWS * (ndp - 1))], g_send.at[XS, m])
            await_bytes(full.at[XS, m], h_send.at[XS, m])

        @pl.when(sec == 1)
        def _():
            await_bytes(full.at[IS, m, pl.ds(0, ROWS * (ndp - 1))], g_send.at[IS, m])
            await_bytes(full.at[IS, m], h_send.at[IS, m])


def flush(*refs):
    arrays = len(refs) // 2
    sems = refs[-1]
    copies = [
        pltpu.make_async_copy(refs[i], refs[arrays + i], sems.at[i]) for i in range(arrays)
    ]
    for copy in copies:
        copy.start()
    for copy in copies:
        copy.wait()


def per_device(ndp, ntensor, inputs, cotangent, scale_exps, up_weight, down_weight):
    nz = ntensor // NY
    micro, own_rows, feats = inputs.shape
    units = up_weight.shape[2]
    half = units // NY
    cut = half // CUTS
    tokens = own_rows * ndp
    vmem = pl.BlockSpec(memory_space=pltpu.VMEM)
    far = pl.BlockSpec(memory_space=pltpu.HBM)
    dma = pltpu.SemaphoreType.DMA
    results = pl.pallas_call(
        functools.partial(kernel, ndp, nz),
        out_shape=[
            jax.ShapeDtypeStruct(inputs.shape, BF),
            jax.ShapeDtypeStruct(inputs.shape, BF),
            jax.ShapeDtypeStruct((feats, units), BF),
            jax.ShapeDtypeStruct((units, feats), BF),
        ],
        in_specs=[far] * 5,
        out_specs=[vmem] * 4,
        scratch_shapes=[
            pltpu.VMEM((NY, feats, half), BF),
            pltpu.VMEM((NY, half, feats), BF),
            pltpu.VMEM((2, micro, tokens, feats), BF),
            pltpu.VMEM((2, micro, 2, CUTS, tokens, cut), BF),
            pltpu.VMEM((2, micro, CUTS, len({1, nz - 1}), ROWS, cut), BF),
            pltpu.VMEM((2, micro, CUTS, tokens, cut), BF),
            pltpu.VMEM((2, micro, CUTS, tokens, cut), BF),
            pltpu.VMEM((2, micro, CUTS, nz - 1, ROWS, cut), BF),
            pltpu.VMEM((2, micro, ROWS, half), F32),
            pltpu.VMEM((2, micro, NY, CUTS, tokens, cut), BF),
            pltpu.VMEM((tokens, feats), F32),
            pltpu.VMEM((2, micro, tokens, feats), BF),
            pltpu.VMEM((2, micro, tokens, feats), BF),
            pltpu.VMEM((2, micro, ROWS, feats), BF),
            pltpu.VMEM((feats, micro * tokens), BF),
            pltpu.SMEM(scale_exps.shape, jnp.int32),
            dma((2, NY)),
            dma((micro,)),
            dma,
            dma((2, micro)),
            dma((2, micro)),
            dma((2, micro)),
            dma((2, micro, CUTS)),
            dma((2, micro)),
            dma((2, micro, CUTS, nz)),
            dma((2, micro)),
            dma((2, micro, CUTS)),
            dma((2, micro)),
            dma((2, micro, CUTS, nz)),
            dma((2, micro, CUTS)),
            dma((2, micro)),
            dma((2, micro)),
            dma((2, micro)),
            dma((2, micro)),
            dma((2, micro)),
            pltpu.SemaphoreType.REGULAR,
        ],
        compiler_params=pltpu.CompilerParams(
            collective_id=0, has_side_effects=True, vmem_limit_bytes=48 * 1024 * 1024
        ),
        name="relay",
    )(*[pltpu.with_memory_space_constraint(a, pltpu.HBM) for a in (inputs, cotangent, scale_exps, up_weight[0], down_weight[0])])
    section_out, input_grads, up_grads, down_grads = pl.pallas_call(
        flush,
        out_shape=[jax.ShapeDtypeStruct(result.shape, result.dtype) for result in results],
        in_specs=[vmem] * 4,
        out_specs=[pl.BlockSpec(memory_space=pl.ANY)] * 4,
        scratch_shapes=[dma((4,))],
        compiler_params=pltpu.CompilerParams(vmem_limit_bytes=1024 * 1024),
        name="flush",
    )(*[pltpu.with_memory_space_constraint(result, pltpu.VMEM) for result in results])
    return section_out[None], input_grads[None], up_grads[None], down_grads[None]


def solution(mesh):
    in_specs = (
        P(None, "dp", "tensor"),
        P(None, "dp", "tensor"),
        P(None, "dp", "tensor"),
        P("section", "tensor", "dp"),
        P("section", "dp", "tensor"),
    )
    out_specs = (
        P("section", None, "dp", "tensor"),
        P("section", None, "dp", "tensor"),
        P("section", "tensor", "dp"),
        P("section", "dp", "tensor"),
    )
    return jax.shard_map(
        functools.partial(per_device, mesh.shape["dp"], mesh.shape["tensor"]),
        mesh=mesh,
        in_specs=in_specs,
        out_specs=out_specs,
        check_vma=False,
    )
```
